256 devices in a mesh: group: 32 (over x, y, core), tp: 8 (over z).
Axes of the slice: x: 4, y: 4, z: 8, core: 2. Of those that a mesh axis runs over, the one named last changes fastest.
Arguments:
- queries_nope: bfloat16 [2, 8192, 8192], P(None, 'group', 'tp'), may hold values from -6 to 6
- queries_rope: bfloat16 [2, 8192, 4096], P(None, 'group', 'tp'), may hold values from -8 to 8
- w_key: bfloat16 [2, 64, 128, 512], P(None, 'tp'), may hold values from -0.5 to 0.5
- w_value: bfloat16 [2, 64, 512, 128], P(None, 'tp'), may hold values from -2.5 to 2.5
- suffix_latent: bfloat16 [2, 8192, 512], P(None, ('group', 'tp')), may hold values from -6 to 6
- suffix_rope: bfloat16 [2, 8192, 64], P(None, ('group', 'tp')), may hold values from -6 to 6
- pool_latent: bfloat16 [2, 512, 64, 512], P(None, 'group'), may hold values from -8 to 8
- pool_rope: bfloat16 [2, 512, 4096], P(None, 'group'), may hold values from -8 to 8
- block_holders: int32 [32, 2, 16], replicated, may hold values from 0 to 31, as said below
- block_ids: int32 [32, 2, 16], replicated, may hold values from 0 to 15
- prefix_blocks: int32 [32, 2], replicated, may hold values from 8 to 16, as said below
Outputs:
- attn_out: bfloat16 [2, 8192, 8192], P(None, 'group', 'tp')
The draws below stay inside these ranges and needn't reach their ends.
Inputs may be any that keep to these rules, and one draw needn't show every extreme that they name: `block_holders`: no entry names the request's own group; at most 2 entries of one group's lists name one holding group, and in every group's lists some holding group is named exactly 2 times. `prefix_blocks`: some request uses all 16 blocks.
All inputs are finite; a program needn't handle non-finite values.
Results may differ from the reference program's by a relative error of at most 0.014.
Values may be sent and summed in bfloat16 or wider, within the bound.
A program may use at most 128 MiB of HBM per device.

```python
import math
import jax
import jax.numpy as jnp
from jax import lax

H = 64
DC = 512
DR = 64
DN = 128
DV = 128
L = 2
BT = 64
R = 2
S = 128
NB = 16
POOL = 16
TOKENS = 8192
BLOCKS = 512
CAP = 2
N_GROUP = 32


def draw_queries_rope(key, part):
    key = jax.random.fold_in(key, 11)
    values = jnp.clip(jax.random.normal(key, (L, TOKENS, H * DR), jnp.float32), -6.0, 6.0)
    return values.astype(jnp.bfloat16)


def draw_pool_rope(key, part):
    key = jax.random.fold_in(key, 12)
    values = jnp.clip(jax.random.normal(key, (L, BLOCKS, BT, DR), jnp.float32), -6.0, 6.0)
    return values.reshape(L, BLOCKS, BT * DR).astype(jnp.bfloat16)


def draw_pool_latent(key, part):
    key = jax.random.fold_in(key, 13)
    values = jax.random.normal(key, (L, BLOCKS, BT, DC), jnp.float32)
    values = jnp.clip(values, -6.0, 6.0)
    return values.astype(jnp.bfloat16)


def draw_block_holders(key, part):
    key = jax.random.fold_in(key, 21)
    slot_count = R * NB
    slot_keys = jax.random.split(jax.random.fold_in(key, 1), N_GROUP)
    slot_perm = jax.vmap(lambda k: jax.random.permutation(k, slot_count))(slot_keys)
    offset_keys = jax.random.split(jax.random.fold_in(key, 2), N_GROUP)
    offset_perm = jax.vmap(lambda k: jax.random.permutation(k, N_GROUP - 1))(offset_keys)
    which = slot_perm // CAP
    offsets = jnp.take_along_axis(offset_perm, which, axis=1)
    holders = (jnp.arange(N_GROUP)[:, None] + 1 + offsets) % N_GROUP
    return holders.reshape(N_GROUP, R, NB).astype(jnp.int32)


def draw_prefix_blocks(key, part):
    key = jax.random.fold_in(key, 31)
    counts = jax.random.randint(key, (N_GROUP * R,), max(1, NB // 2), NB + 1)
    chosen = jax.random.randint(jax.random.fold_in(key, 1), (), 0, N_GROUP * R)
    counts = jnp.where(jnp.arange(N_GROUP * R) == chosen, NB, counts)
    return counts.reshape(N_GROUP, R).astype(jnp.int32)


def touch_ends(array, rng, least, high):
    index_at = [jax.random.randint(jax.random.fold_in(rng, axis), (), 0, length) for axis, length in enumerate(array.shape)]
    longest = array.shape.index(max(array.shape))
    neighbour = index_at[:longest] + [(index_at[longest] + 1) % array.shape[longest]] + index_at[longest + 1:]
    return array.at[tuple(index_at)].set(least).at[tuple(neighbour)].set(high)


def shard_levels(rng, dims, shards, low, high):
    loudness = 1.0
    for axis_at, shards_of in shards:
        draws = jax.random.uniform(jax.random.fold_in(jax.random.fold_in(rng, 6), axis_at), (shards_of,), jnp.float32, low / len(shards), high / len(shards))
        loudness = loudness * jnp.repeat(jnp.exp(draws), dims[axis_at] // shards_of).reshape((-1,) + (1,) * (len(dims) - 1 - axis_at))
    return loudness


def scatter_about(stream_key, dims, width, limit, shards=(), kind=jnp.bfloat16):
    entries = width * jax.random.normal(stream_key, dims, jnp.float32)
    if shards:
        entries = entries * shard_levels(stream_key, dims, shards, -0.22, 0.18)
    return jnp.clip(entries, -limit, limit).astype(kind)


def setup_inputs(seed: int = 0) -> dict:
    streams_of = jax.random.split(jax.random.key(seed), 12)
    queries_nope = scatter_about(streams_of[0], (L, TOKENS, H * DN), 1.0, 6.0, ((1, 32), (2, 8)))
    queries_rope = draw_queries_rope(jax.random.fold_in(streams_of[11], 71), 0)
    w_key = scatter_about(streams_of[2], (L, H, DN, DC), DN ** -0.5, 0.5, ((1, 8),))
    w_value = scatter_about(streams_of[3], (L, H, DC, DV), (4.0 / DC ** 0.5), 2.5, ((1, 8),))
    suffix_latent = scatter_about(streams_of[4], (L, TOKENS, DC), 1.0, 6.0, ((1, 256),))
    suffix_rope = scatter_about(streams_of[5], (L, TOKENS, DR), 1.0, 6.0, ((1, 256),))
    pool_latent = draw_pool_latent(jax.random.fold_in(streams_of[11], 71), 0)
    pool_rope = draw_pool_rope(jax.random.fold_in(streams_of[11], 71), 0)
    block_holders = draw_block_holders(jax.random.fold_in(streams_of[11], 71), 0)
    block_ids = touch_ends(jax.random.randint(streams_of[9], (N_GROUP, R, NB), 0, POOL), jax.random.fold_in(streams_of[9], 1), 0, POOL - 1).astype(jnp.int32)
    prefix_blocks = draw_prefix_blocks(jax.random.fold_in(streams_of[11], 71), 0)
    return {"queries_nope": queries_nope, "queries_rope": queries_rope, "w_key": w_key, "w_value": w_value, "suffix_latent": suffix_latent, "suffix_rope": suffix_rope, "pool_latent": pool_latent, "pool_rope": pool_rope, "block_holders": block_holders, "block_ids": block_ids, "prefix_blocks": prefix_blocks}


def attend_group(absorbed, query_rope, keys_latent, keys_rope, counts, value_weight):
    wide = jnp.float32
    scores = jnp.einsum('rshc,rkc->rshk', absorbed.astype(wide), keys_latent.astype(wide))
    scores = scores + jnp.einsum('rshd,rkd->rshk', query_rope.astype(wide), keys_rope.astype(wide))
    scores = scores * (1.0 / math.sqrt(DN + DR))
    prefix_len = NB * BT
    positions = jnp.arange(NB * BT + S, dtype=jnp.int32)
    query_rows = jnp.arange(S, dtype=jnp.int32)
    live_prefix = (positions[None, :] < prefix_len) & (positions[None, :] // BT < counts[:, None])
    live_suffix = (positions[None, :] >= prefix_len) & (positions[None, :] - prefix_len <= query_rows[:, None])
    live_keys = live_prefix[:, None, None, :] | live_suffix[None, :, None, :]
    scores = jnp.where(live_keys, scores, -jnp.inf)
    attention = jax.nn.softmax(scores, axis=-1).astype(jnp.bfloat16)
    context = jnp.einsum('rshk,rkc->rshc', attention.astype(wide), keys_latent.astype(wide)).astype(jnp.bfloat16)
    return jnp.einsum('rshc,hcv->rshv', context.astype(wide), value_weight.astype(wide)).astype(jnp.bfloat16)

def reference(queries_nope, queries_rope, w_key, w_value, suffix_latent, suffix_rope, pool_latent, pool_rope, block_holders, block_ids, prefix_blocks):
    holders = block_holders.reshape(N_GROUP, R * NB)
    block_list = block_ids.reshape(N_GROUP, R * NB)
    results = []
    for layer_index in range(L):
        latent_pool = pool_latent[layer_index].reshape(N_GROUP, POOL, BT, DC)
        rope_pool = pool_rope[layer_index].reshape(N_GROUP, POOL, BT, DR)

        def one_group(group_id):
            holder_row = holders[group_id]
            block_row = block_list[group_id]
            prefix_latent = latent_pool[holder_row, block_row].reshape(R, NB * BT, DC)
            prefix_rope = rope_pool[holder_row, block_row].reshape(R, NB * BT, DR)
            first_row = (group_id * (R * S)).astype(jnp.int32)
            suffix_lat = lax.dynamic_slice_in_dim(suffix_latent[layer_index], first_row, R * S, 0).reshape(R, S, DC)
            suffix_rp = lax.dynamic_slice_in_dim(suffix_rope[layer_index], first_row, R * S, 0).reshape(R, S, DR)
            keys_latent = jnp.concatenate([prefix_latent, suffix_lat], axis=1)
            keys_rope = jnp.concatenate([prefix_rope, suffix_rp], axis=1)
            nope_rows = lax.dynamic_slice_in_dim(queries_nope[layer_index], first_row, R * S, 0).reshape(R * S, H, DN)
            absorbed = jnp.einsum('thn,hnc->thc', nope_rows.astype(jnp.float32), w_key[layer_index].astype(jnp.float32)).astype(jnp.bfloat16)
            rope_rows = lax.dynamic_slice_in_dim(queries_rope[layer_index], first_row, R * S, 0).reshape(R, S, H, DR)
            heads_out = attend_group(absorbed.reshape(R, S, H, DC), rope_rows, keys_latent, keys_rope, prefix_blocks[group_id], w_value[layer_index])
            return heads_out.reshape(R * S, H * DV)
        grouped = lax.map(one_group, jnp.arange(N_GROUP, dtype=jnp.int32))
        results.append(grouped.reshape(TOKENS, H * DV))
    return jnp.stack(results)
```

```python
import functools
import math

import jax
import jax.numpy as jnp
from jax import lax
from jax.experimental import pallas as pl
from jax.experimental.pallas import tpu as pltpu
from jax.sharding import PartitionSpec as P

MESH = pl.DeviceIdType.MESH
BF16 = jnp.bfloat16
F32 = jnp.float32
CAP = 2
QUARTERS = 4


def dot(a, b):
    return jnp.dot(a, b, preferred_element_type=F32)


def dot_t(a, b):
    return lax.dot_general(a, b, (((1,), (1,)), ((), ())), preferred_element_type=F32)


def kernel(
    dims,
    ids,
    places,
    counts,
    qn_in,
    qr_in,
    wk_in,
    wv_in,
    sl_in,
    sr_in,
    pool_in,
    prope_in,
    out,
    qn,
    qr,
    wk,
    wv,
    pool0,
    pool1,
    prope,
    send0,
    send1,
    got0,
    got1,
    keys0,
    keys1,
    suf_lat,
    suf_rope,
    absorbed,
    qrope,
    in_sem,
    xy_send,
    xy_recv,
    suf_send,
    suf_recv,
    hop1_send,
    hop1_recv,
    hop2_send,
    hop2_recv,
):
    groups, tps, requests, blocks, suffix, heads, dc, dr, dn, dv = dims
    g_me = lax.axis_index("group")
    t_me = lax.axis_index("tp")
    right = lax.rem(t_me + 1, tps)
    left = lax.rem(t_me + tps - 1, tps)
    quarter = lax.rem(t_me, QUARTERS)
    q_left = lax.rem(quarter + QUARTERS - 1, QUARTERS)
    q_right = lax.rem(quarter + 1, QUARTERS)
    q_far = lax.rem(quarter + 2, QUARTERS)
    piece = 16
    seg = blocks * piece
    half = seg // 2
    rows = requests * suffix // tps
    pairs = heads // 2
    layers = 2
    scale = 1.0 / math.sqrt(dn + dr)

    first = pl.multiple_of(quarter * piece, piece)
    mine = pl.ds(pl.multiple_of(t_me * rows, rows), rows)
    loads = [
        pltpu.make_async_copy(pool_in.at[0, :, pl.ds(first, piece)], pool0, in_sem.at[0]),
        pltpu.make_async_copy(prope_in, prope, in_sem.at[1]),
        pltpu.make_async_copy(pool_in.at[1, :, pl.ds(first, piece)], pool1, in_sem.at[2]),
        pltpu.make_async_copy(sl_in, suf_lat.at[:, mine], in_sem.at[3]),
        pltpu.make_async_copy(sr_in, suf_rope.at[mine], in_sem.at[4]),
        pltpu.make_async_copy(qn_in, qn, in_sem.at[5]),
        pltpu.make_async_copy(wk_in, wk, in_sem.at[6]),
        pltpu.make_async_copy(qr_in, qr, in_sem.at[7]),
        pltpu.make_async_copy(wv_in, wv, in_sem.at[8]),
    ]
    for load in loads:
        load.start()

    barrier = pltpu.get_barrier_semaphore()

    def greet_group(i, carry):
        pl.semaphore_signal(
            barrier, inc=1, device_id={"group": lax.rem(g_me + i, groups)}, device_id_type=MESH
        )
        return carry

    def greet_tp(i, carry):
        pl.semaphore_signal(
            barrier, inc=1, device_id={"tp": lax.rem(t_me + i, tps)}, device_id_type=MESH
        )
        return carry

    lax.fori_loop(1, groups, greet_group, 0)
    lax.fori_loop(1, tps, greet_tp, 0)
    loads[0].wait()
    loads[1].wait()
    pl.semaphore_wait(barrier, groups + tps - 2)

    def plane_copy(layer, g):
        src, dst = ((send0, got0), (send1, got1))[layer]
        return pltpu.make_async_remote_copy(
            src_ref=src.at[g],
            dst_ref=dst.at[g_me],
            send_sem=xy_send.at[layer],
            recv_sem=xy_recv.at[layer],
            device_id={"group": g},
            device_id_type=MESH,
        )

    def fill0(i, carry):
        g = lax.rem(g_me + i, groups)
        for k in range(CAP):
            b = ids[g, k]
            send0[g, k, :, :dc] = pool0[b]
            send0[g, k, :, dc:] = prope[b]
        plane_copy(0, g).start()
        return carry

    lax.fori_loop(1, groups, fill0, 0)

    loads[3].wait()
    loads[4].wait()

    def suffix_copies(i):
        peer = lax.rem(t_me + i, tps)
        return [
            pltpu.make_async_remote_copy(
                src_ref=suf_lat.at[:, mine],
                dst_ref=suf_lat.at[:, mine],
                send_sem=suf_send.at[0],
                recv_sem=suf_recv.at[0],
                device_id={"tp": peer},
                device_id_type=MESH,
            ),
            pltpu.make_async_remote_copy(
                src_ref=suf_rope.at[mine],
                dst_ref=suf_rope.at[mine],
                send_sem=suf_send.at[1],
                recv_sem=suf_recv.at[1],
                device_id={"tp": peer},
                device_id_type=MESH,
            ),
        ]

    def send_suffix(i, carry):
        for copy in suffix_copies(i):
            copy.start()
        return carry

    lax.fori_loop(1, tps, send_suffix, 0)

    loads[2].wait()

    def fill1(i, carry):
        g = lax.rem(g_me + i, groups)
        for k in range(CAP):
            send1[g, k] = pool1[ids[g, k]]
        return carry

    lax.fori_loop(1, groups, fill1, 0)
    for k in range(CAP):
        got0[g_me, k] = jnp.zeros((piece, dc + 2 * dr), BF16)
        got1[g_me, k] = jnp.zeros((piece, dc), BF16)

    loads[5].wait()
    loads[6].wait()
    loads[7].wait()
    lane = lax.broadcasted_iota(jnp.int32, (suffix, 2 * dr), 1)

    def absorb(hp, carry):
        for layer in range(layers):
            for j in range(2):
                at = pl.ds(pl.multiple_of((hp * 2 + j) * dn, dn), dn)
                a = dot(qn[layer, :, at], wk[layer, hp * 2 + j]).astype(BF16)
                for r in range(requests):
                    absorbed[layer, r, hp, j * suffix : (j + 1) * suffix] = a[
                        r * suffix : (r + 1) * suffix
                    ]
            at = pl.ds(pl.multiple_of(hp * 2 * dr, 2 * dr), 2 * dr)
            for r in range(requests):
                both = qr[layer, r * suffix : (r + 1) * suffix, at].astype(F32)
                swapped = pltpu.roll(both, dr, 1)
                even, odd = (both, swapped) if layer == 0 else (swapped, both)
                live = (lane < dr) if layer == 0 else (lane >= dr)
                qrope[layer, r, hp, :suffix] = jnp.where(live, even, 0.0).astype(BF16)
                qrope[layer, r, hp, suffix:] = jnp.where(live, odd, 0.0).astype(BF16)
        return carry

    lax.fori_loop(0, pairs, absorb, 0)

    keys = (keys0, keys1)
    got = (got0, got1)

    def plane_wait(layer):
        pltpu.make_async_copy(
            got[layer].at[pl.ds(1, groups - 1)],
            got[layer].at[pl.ds(1, groups - 1)],
            xy_recv.at[layer],
        ).wait()

    def compact(layer):
        def one(b, carry):
            for r in range(requests):
                place = places[r * blocks + b]
                keys[layer][quarter, r, pl.ds(pl.multiple_of(b * piece, piece), piece)] = got[
                    layer
                ][place // CAP, place % CAP]
            return carry

        lax.fori_loop(0, blocks, one, 0)

    def ring_copy(ref, hop, unit, way):
        sems = ((hop1_send, hop1_recv), (hop2_send, hop2_recv))[hop]
        return pltpu.make_async_remote_copy(
            src_ref=ref,
            dst_ref=ref,
            send_sem=sems[0].at[unit, way],
            recv_sem=sems[1].at[unit, way],
            device_id={"tp": (right, left)[way]},
            device_id_type=MESH,
        )

    def hop1(layer, r, way):
        return ring_copy(keys[layer].at[quarter, r], 0, layer * requests + r, way)

    def hop1_in(layer, r, way):
        ref = keys[layer].at[(q_left, q_right)[way], r]
        return ring_copy(ref, 0, layer * requests + r, way)

    def hop2(layer, r, way):
        ref = keys[layer].at[(q_left, q_right)[way], r, pl.ds(way * half, half)]
        return ring_copy(ref, 1, layer * requests + r, way)

    def hop2_in(layer, r, way):
        ref = keys[layer].at[q_far, r, pl.ds(way * half, half)]
        return ring_copy(ref, 1, layer * requests + r, way)

    def forward(layer, r):
        for way in range(2):
            hop1_in(layer, r, way).wait_recv()
            hop2(layer, r, way).start()

    def arrived(layer, r):
        for way in range(2):
            hop2_in(layer, r, way).wait_recv()

    def send_ring(layer):
        for r in range(requests):
            for way in range(2):
                hop1(layer, r, way).start()

    def attend(layer, r):
        key_at = lax.broadcasted_iota(jnp.int32, (2 * suffix, seg), 1)
        live_prefix = key_at < counts[r] * piece
        query_at = lax.rem(lax.broadcasted_iota(jnp.int32, (2 * suffix, suffix), 0), suffix)
        live_suffix = lax.broadcasted_iota(jnp.int32, (2 * suffix, suffix), 1) <= query_at
        suffix_rows = slice(r * suffix, (r + 1) * suffix)

        def one(hp, carry):
            a = absorbed[layer, r, hp]
            qp = qrope[layer, r, hp]
            scores = []
            for q in range(QUARTERS):
                s = dot_t(a, keys[layer][q, r, :, :dc]) + dot_t(qp, keys0[q, r, :, dc:])
                scores.append(jnp.where(live_prefix, s * scale, -jnp.inf))
            s = dot_t(a, suf_lat[layer, suffix_rows]) + dot_t(qp, suf_rope[suffix_rows])
            last = jnp.where(live_suffix, s * scale, -jnp.inf)
            top = functools.reduce(jnp.maximum, scores).max(axis=1, keepdims=True)
            top = jnp.maximum(top, last.max(axis=1, keepdims=True))
            probs = [jnp.exp(s - top) for s in scores]
            last = jnp.exp(last - top)
            total = sum(probs).sum(axis=1, keepdims=True) + last.sum(axis=1, keepdims=True)
            context = dot(last.astype(BF16), suf_lat[layer, suffix_rows])
            for q in range(QUARTERS):
                context = context + dot(probs[q].astype(BF16), keys[layer][q, r, :, :dc])
            context = (context / total).astype(BF16)
            for j in range(2):
                h = hp * 2 + j
                out[layer, suffix_rows, pl.ds(pl.multiple_of(h * dv, dv), dv)] = dot(
                    context[j * suffix : (j + 1) * suffix], wv[layer, h]
                ).astype(BF16)
            return carry

        lax.fori_loop(0, pairs, one, 0)

    plane_wait(0)
    compact(0)

    def send1_step(i, carry):
        plane_copy(1, lax.rem(g_me + i, groups)).start()
        return carry

    send_ring(0)
    lax.fori_loop(1, groups, send1_step, 0)
    pltpu.make_async_copy(
        suf_lat.at[:, pl.ds(0, rows * (tps - 1))],
        suf_lat.at[:, pl.ds(0, rows * (tps - 1))],
        suf_recv.at[0],
    ).wait()
    pltpu.make_async_copy(
        suf_rope.at[pl.ds(0, rows * (tps - 1))],
        suf_rope.at[pl.ds(0, rows * (tps - 1))],
        suf_recv.at[1],
    ).wait()
    loads[8].wait()
    forward(0, 0)
    forward(0, 1)
    plane_wait(1)
    compact(1)
    send_ring(1)
    arrived(0, 0)
    attend(0, 0)
    forward(1, 0)
    arrived(0, 1)
    attend(0, 1)
    forward(1, 1)
    arrived(1, 0)
    attend(1, 0)
    arrived(1, 1)
    attend(1, 1)

    for layer in range(layers):
        pltpu.make_async_copy(
            (send0, send1)[layer].at[pl.ds(1, groups - 1)],
            (send0, send1)[layer].at[pl.ds(1, groups - 1)],
            xy_send.at[layer],
        ).wait()
        for r in range(requests):
            for way in range(2):
                hop1(layer, r, way).wait_send()
                hop2(layer, r, way).wait_send()
    pltpu.make_async_copy(
        suf_lat.at[:, pl.ds(0, rows * (tps - 1))],
        suf_lat.at[:, pl.ds(0, rows * (tps - 1))],
        suf_send.at[0],
    ).wait()
    pltpu.make_async_copy(
        suf_rope.at[pl.ds(0, rows * (tps - 1))],
        suf_rope.at[pl.ds(0, rows * (tps - 1))],
        suf_send.at[1],
    ).wait()


def slot_tables(block_holders, block_ids, groups, own_group):
    slots = block_holders.shape[1] * block_holders.shape[2]
    holders = block_holders.reshape(groups, slots)
    block_list = block_ids.reshape(groups, slots)
    order = jnp.arange(slots, dtype=jnp.int32)
    match = holders == own_group
    first = jnp.min(jnp.where(match, order, slots), axis=1, keepdims=True)
    final = jnp.max(jnp.where(match, order, -1), axis=1, keepdims=True)
    at = jnp.stack([order == first, order == final], axis=1)
    send_ids = jnp.sum(jnp.where(at, block_list[:, None, :], 0), axis=2)
    own = lax.dynamic_index_in_dim(holders, own_group, 0, keepdims=False)
    earlier = (own[None, :] == own[:, None]) & (order[None, :] < order[:, None])
    places = own * CAP + jnp.sum(earlier.astype(jnp.int32), axis=1)
    return send_ids, places


def per_device(
    queries_nope,
    queries_rope,
    w_key,
    w_value,
    suffix_latent,
    suffix_rope,
    pool_latent,
    pool_rope,
    block_holders,
    block_ids,
    prefix_blocks,
):
    groups = lax.axis_size("group")
    tps = lax.axis_size("tp")
    own_group = lax.axis_index("group")
    requests, blocks = block_holders.shape[1:]
    layers, tokens = queries_nope.shape[:2]
    suffix = tokens // requests
    heads, dn, dc = w_key.shape[1:]
    dv = w_value.shape[3]
    dr = suffix_rope.shape[2]
    held, length = pool_latent.shape[1:3]
    piece = length // QUARTERS
    seg = blocks * piece
    rows = suffix_latent.shape[1]
    ids, places = slot_tables(block_holders, block_ids, groups, own_group)
    counts = lax.dynamic_index_in_dim(prefix_blocks, own_group, 0, keepdims=False)
    quarter = lax.rem(lax.axis_index("tp"), QUARTERS)
    prope = lax.dynamic_slice_in_dim(pool_rope, quarter * piece * dr, piece * dr, 2)
    prope = prope.reshape(layers, held, piece, dr)
    prope = jnp.concatenate([prope[0], prope[1]], axis=-1)
    srope = jnp.concatenate([suffix_rope[0], suffix_rope[1]], axis=-1)
    dims = (groups, tps, requests, blocks, suffix, heads, dc, dr, dn, dv)
    smem = pl.BlockSpec(memory_space=pltpu.SMEM)
    hbm = pl.BlockSpec(memory_space=pl.ANY)
    units = layers * requests
    return pl.pallas_call(
        functools.partial(kernel, dims),
        out_shape=jax.ShapeDtypeStruct((layers, tokens, heads * dv), BF16),
        in_specs=[smem] * 3 + [hbm] * 8,
        out_specs=pl.BlockSpec(memory_space=pltpu.VMEM),
        scratch_shapes=[
            pltpu.VMEM(queries_nope.shape, BF16),
            pltpu.VMEM(queries_rope.shape, BF16),
            pltpu.VMEM(w_key.shape, BF16),
            pltpu.VMEM(w_value.shape, BF16),
            pltpu.VMEM((held, piece, dc), BF16),
            pltpu.VMEM((held, piece, dc), BF16),
            pltpu.VMEM((held, piece, 2 * dr), BF16),
            pltpu.VMEM((groups, CAP, piece, dc + 2 * dr), BF16),
            pltpu.VMEM((groups, CAP, piece, dc), BF16),
            pltpu.VMEM((groups, CAP, piece, dc + 2 * dr), BF16),
            pltpu.VMEM((groups, CAP, piece, dc), BF16),
            pltpu.VMEM((QUARTERS, requests, seg, dc + 2 * dr), BF16),
            pltpu.VMEM((QUARTERS, requests, seg, dc), BF16),
            pltpu.VMEM((layers, rows * tps, dc), BF16),
            pltpu.VMEM((rows * tps, 2 * dr), BF16),
            pltpu.VMEM((layers, requests, heads // 2, 2 * suffix, dc), BF16),
            pltpu.VMEM((layers, requests, heads // 2, 2 * suffix, 2 * dr), BF16),
            pltpu.SemaphoreType.DMA((9,)),
            pltpu.SemaphoreType.DMA((layers,)),
            pltpu.SemaphoreType.DMA((layers,)),
            pltpu.SemaphoreType.DMA((2,)),
            pltpu.SemaphoreType.DMA((2,)),
            pltpu.SemaphoreType.DMA((units, 2)),
            pltpu.SemaphoreType.DMA((units, 2)),
            pltpu.SemaphoreType.DMA((units, 2)),
            pltpu.SemaphoreType.DMA((units, 2)),
        ],
        compiler_params=pltpu.CompilerParams(
            collective_id=0, has_side_effects=True, vmem_limit_bytes=56 * 1024 * 1024
        ),
        cost_estimate=pl.CostEstimate(
            flops=12_000_000_000, bytes_accessed=12_000_000, transcendentals=5_000_000
        ),
    )(
        ids,
        places,
        counts,
        queries_nope,
        queries_rope,
        w_key,
        w_value,
        suffix_latent,
        srope,
        pool_latent,
        prope,
    )


def solution(mesh):
    in_specs = (
        P(None, "group", "tp"),
        P(None, "group", "tp"),
        P(None, "tp", None, None),
        P(None, "tp", None, None),
        P(None, ("group", "tp"), None),
        P(None, ("group", "tp"), None),
        P(None, "group", None, None),
        P(None, "group", None),
        P(),
        P(),
        P(),
    )
    out_specs = P(None, "group", "tp")
    return jax.shard_map(
        per_device, mesh=mesh, in_specs=in_specs, out_specs=out_specs, check_vma=False
    )
```

```python
import functools
import math

import jax
import jax.numpy as jnp
from jax import lax
from jax.experimental import pallas as pl
from jax.experimental.pallas import tpu as pltpu
from jax.sharding import PartitionSpec as P

MESH = pl.DeviceIdType.MESH
BF16 = jnp.bfloat16
F32 = jnp.float32
CAP = 2
QUARTERS = 4


def dot(a, b):
    return jnp.dot(a, b, preferred_element_type=F32)


def dot_t(a, b):
    return lax.dot_general(a, b, (((1,), (1,)), ((), ())), preferred_element_type=F32)


def torus_peer(g_me, groups, i):
    if groups != 32:
        return lax.rem(g_me + i, groups)
    x, y, c = g_me // 8, lax.rem(g_me // 2, 4), lax.rem(g_me, 2)
    x = lax.rem(x + i, 4)
    y = lax.rem(y + i + i // 4, 4)
    c = lax.rem(c + i // 16, 2)
    return x * 8 + y * 2 + c


def kernel(
    dims,
    holders,
    block_ids,
    prefix_blocks,
    qn_in,
    qr_in,
    wk_in,
    wv_in,
    sl_in,
    sr_in,
    pool_in,
    prope_in,
    out,
    qn,
    qr,
    wk,
    wv,
    pools,
    prope_lanes,
    prope_wide,
    prope,
    srope,
    sends,
    gots,
    keys,
    sufs,
    absorbed,
    qrope,
    picks,
    ranks,
    in_sem,
    xy_send,
    xy_recv,
    suf_send,
    suf_recv,
    hop1_send,
    hop1_recv,
    hop2_send,
    hop2_recv,
):
    groups, tps, requests, blocks, suffix, heads, dc, dr, dn, dv = dims
    g_me = lax.axis_index("group")
    t_me = lax.axis_index("tp")
    right = lax.rem(t_me + 1, tps)
    left = lax.rem(t_me + tps - 1, tps)
    quarter = lax.rem(t_me, QUARTERS)
    q_left = lax.rem(quarter + QUARTERS - 1, QUARTERS)
    q_right = lax.rem(quarter + 1, QUARTERS)
    q_far = lax.rem(quarter + 2, QUARTERS)
    piece = 16
    seg = blocks * piece
    half = seg // 2
    rows = requests * suffix // tps
    pairs = heads // 2
    layers = 2
    hw = dc // 2
    scale = math.log2(math.e) / math.sqrt(dn + dr)

    first = pl.multiple_of(quarter * piece, piece)
    lanes = pl.ds(pl.multiple_of(quarter * piece * dr, piece * dr), piece * dr)
    tokens = pl.ds(first, piece)
    mine = pl.ds(pl.multiple_of(t_me * rows, rows), rows)
    loads = [
        pltpu.make_async_copy(pool_in.at[0, :, tokens, pl.ds(0, hw)], pools[0], in_sem.at[0]),
        pltpu.make_async_copy(sl_in.at[0], sufs[0].at[mine, pl.ds(0, dc)], in_sem.at[1]),
        pltpu.make_async_copy(sl_in.at[1], sufs[1].at[mine], in_sem.at[2]),
        pltpu.make_async_copy(sr_in, srope, in_sem.at[3]),
        pltpu.make_async_copy(pool_in.at[0, :, tokens, pl.ds(hw, hw)], pools[1], in_sem.at[4]),
        pltpu.make_async_copy(prope_in.at[:, :, lanes], prope_lanes, in_sem.at[5]),
        pltpu.make_async_copy(pool_in.at[1, :, tokens, pl.ds(0, hw)], pools[2], in_sem.at[6]),
        pltpu.make_async_copy(pool_in.at[1, :, tokens, pl.ds(hw, hw)], pools[3], in_sem.at[7]),
        pltpu.make_async_copy(qn_in, qn, in_sem.at[8]),
        pltpu.make_async_copy(wk_in, wk, in_sem.at[9]),
        pltpu.make_async_copy(qr_in, qr, in_sem.at[10]),
        pltpu.make_async_copy(wv_in, wv, in_sem.at[11]),
    ]
    for load in loads:
        load.start()

    barrier = pltpu.get_barrier_semaphore()

    def greet(i, carry):
        pl.semaphore_signal(
            barrier, inc=1, device_id={"group": torus_peer(g_me, groups, i)}, device_id_type=MESH
        )
        return carry

    for neighbour in (left, right):
        pl.semaphore_signal(barrier, inc=1, device_id={"tp": neighbour}, device_id_type=MESH)
    lax.fori_loop(1, groups, greet, 0)

    slots = [(r, j) for r in range(requests) for j in range(blocks)]

    def table(i, carry):
        g = torus_peer(g_me, groups, i)
        listed = [holders[g, r, j] == g_me for r, j in slots]
        names = [block_ids[g, r, j] for r, j in slots]
        final = jnp.int32(0)
        for m, b in zip(listed, names):
            final = jnp.where(m, b, final)
        early = jnp.int32(0)
        for m, b in zip(listed[::-1], names[::-1]):
            early = jnp.where(m, b, early)
        picks[g, 0] = early
        picks[g, 1] = final
        return carry

    def fill(c):
        def one(i, carry):
            g = torus_peer(g_me, groups, i)
            for k in range(CAP):
                b = picks[g, k]
                if c == 1:
                    sends[c][g, k, :, :hw] = pools[c][b]
                    sends[c][g, k, :, hw:] = prope[b]
                else:
                    sends[c][g, k] = pools[c][b]
            return carry

        lax.fori_loop(1, groups, one, 0)

    def plane_copy(c, g):
        return pltpu.make_async_remote_copy(
            src_ref=sends[c].at[g],
            dst_ref=gots[c].at[g_me],
            send_sem=xy_send.at[c],
            recv_sem=xy_recv.at[c],
            device_id={"group": g},
            device_id_type=MESH,
        )

    def plane_send(c):
        def one(i, carry):
            plane_copy(c, torus_peer(g_me, groups, i)).start()
            return carry

        lax.fori_loop(1, groups, one, 0)

    def others(ref):
        return ref.at[pl.ds(1, groups - 1)]

    def plane_wait(c):
        pltpu.make_async_copy(others(gots[c]), others(gots[c]), xy_recv.at[c]).wait()

    def suffix_copy(h, way, layer, arriving):
        step = h + 1 if arriving else h
        origin = lax.rem(t_me + (tps - step if way == 0 else step), tps)
        ref = sufs[layer].at[pl.ds(pl.multiple_of(origin * rows, rows), rows)]
        return pltpu.make_async_remote_copy(
            src_ref=ref,
            dst_ref=ref,
            send_sem=suf_send.at[h, way, layer],
            recv_sem=suf_recv.at[h, way, layer],
            device_id={"tp": (right, left)[way]},
            device_id_type=MESH,
        )

    last_hop = tps // 2 - 1

    def carried(h, way):
        return (0, 1) if h < last_hop else (way,)

    def suffix_send(h):
        for way in range(2):
            for layer in carried(h, way):
                suffix_copy(h, way, layer, False).start()

    def suffix_wait(h):
        for way in range(2):
            for layer in carried(h, way):
                suffix_copy(h, way, layer, True).wait_recv()

    def suffix_forward(h):
        suffix_wait(h - 1)
        suffix_send(h)

    lax.fori_loop(1, groups, table, 0)
    loads[0].wait()
    fill(0)
    for at in (1, 2, 3):
        loads[at].wait()
    sufs[0][mine, dc:] = jnp.concatenate(
        [srope[0].astype(F32), srope[1].astype(F32)], axis=1
    ).astype(BF16)
    pl.semaphore_wait(barrier, groups + 1)
    plane_send(0)
    suffix_send(0)

    loads[4].wait()
    loads[5].wait()
    held = prope.shape[0]
    low = lax.broadcasted_iota(jnp.int32, (held, 2 * dr), 1) < dr
    for j in range(piece // 2):
        x0 = prope_lanes[0, :, 2 * dr * j : 2 * dr * (j + 1)].astype(F32)
        x1 = prope_lanes[1, :, 2 * dr * j : 2 * dr * (j + 1)].astype(F32)
        prope_wide[:, 2 * j, :] = jnp.where(low, x0, pltpu.roll(x1, dr, 1))
        prope_wide[:, 2 * j + 1, :] = jnp.where(low, pltpu.roll(x0, dr, 1), x1)
    prope[...] = prope_wide[...].astype(BF16)
    fill(1)
    plane_send(1)

    own = [holders[g_me, r, j] for r, j in slots]
    for s, (r, j) in enumerate(slots):
        rank = jnp.int32(0)
        for h in own[:s]:
            rank = jnp.where(h == own[s], 1, rank)
        ranks[r, j] = rank
    for c in range(4):
        for k in range(CAP):
            gots[c][g_me, k] = jnp.zeros(gots[c].shape[2:], BF16)

    lane = lax.broadcasted_iota(jnp.int32, (suffix, 2 * dr), 1)

    def absorb(layer):
        def one(hp, carry):
            for j in range(2):
                at = pl.ds(pl.multiple_of((hp * 2 + j) * dn, dn), dn)
                a = dot(qn[layer, :, at], wk[layer, hp * 2 + j]).astype(BF16)
                for r in range(requests):
                    absorbed[layer, r, hp, j * suffix : (j + 1) * suffix] = a[
                        r * suffix : (r + 1) * suffix
                    ]
            at = pl.ds(pl.multiple_of(hp * 2 * dr, 2 * dr), 2 * dr)
            for r in range(requests):
                both = qr[layer, r * suffix : (r + 1) * suffix, at].astype(F32)
                swapped = pltpu.roll(both, dr, 1)
                even, odd = (both, swapped) if layer == 0 else (swapped, both)
                live = (lane < dr) if layer == 0 else (lane >= dr)
                qrope[layer, r, hp, :suffix] = jnp.where(live, even, 0.0).astype(BF16)
                qrope[layer, r, hp, suffix:] = jnp.where(live, odd, 0.0).astype(BF16)
            return carry

        lax.fori_loop(0, pairs, one, 0)

    def compact(c):
        def one(b, carry):
            for r in range(requests):
                at = pl.ds(pl.multiple_of(b * piece, piece), piece)
                keys[c][quarter, r, at] = gots[c][holders[g_me, r, b], ranks[r, b]]
            return carry

        lax.fori_loop(0, blocks, one, 0)

    def ring_copy(ref, hop, unit, way):
        sems = ((hop1_send, hop1_recv), (hop2_send, hop2_recv))[hop]
        return pltpu.make_async_remote_copy(
            src_ref=ref,
            dst_ref=ref,
            send_sem=sems[0].at[unit, way],
            recv_sem=sems[1].at[unit, way],
            device_id={"tp": (right, left)[way]},
            device_id_type=MESH,
        )

    def hop1(c, r, way):
        return ring_copy(keys[c].at[quarter, r], 0, c * requests + r, way)

    def hop1_in(c, r, way):
        return ring_copy(keys[c].at[(q_left, q_right)[way], r], 0, c * requests + r, way)

    def hop2(c, r, way):
        ref = keys[c].at[(q_left, q_right)[way], r, pl.ds(way * half, half)]
        return ring_copy(ref, 1, c * requests + r, way)

    def hop2_in(c, r, way):
        ref = keys[c].at[q_far, r, pl.ds(way * half, half)]
        return ring_copy(ref, 1, c * requests + r, way)

    def ring_send(c, r):
        for way in range(2):
            hop1(c, r, way).start()

    def forward(c, r):
        for way in range(2):
            hop1_in(c, r, way).wait_recv()
            hop2(c, r, way).start()

    def arrived(c, r):
        for way in range(2):
            hop2_in(c, r, way).wait_recv()

    def attend(layer, r, begin, end):
        ka, kb = keys[2 * layer], keys[2 * layer + 1]
        key_at = lax.broadcasted_iota(jnp.int32, (2 * suffix, seg), 1)
        live_prefix = key_at < prefix_blocks[g_me, r] * piece
        query_at = lax.rem(lax.broadcasted_iota(jnp.int32, (2 * suffix, suffix), 0), suffix)
        live_suffix = lax.broadcasted_iota(jnp.int32, (2 * suffix, suffix), 1) <= query_at
        suffix_rows = slice(r * suffix, (r + 1) * suffix)

        def one(hp, carry):
            a = absorbed[layer, r, hp]
            qp = qrope[layer, r, hp]
            scores = []
            for q in range(QUARTERS):
                s = dot_t(a[:, :hw], ka[q, r]) + dot_t(a[:, hw:], kb[q, r, :, :hw])
                s = s + dot_t(qp, keys[1][q, r, :, hw:])
                scores.append(jnp.where(live_prefix, s, -jnp.inf))
            s = dot_t(a, sufs[layer][suffix_rows, :dc]) + dot_t(qp, sufs[0][suffix_rows, dc:])
            last = jnp.where(live_suffix, s, -jnp.inf)
            top = functools.reduce(jnp.maximum, scores).max(axis=1, keepdims=True)
            top = jnp.maximum(top, last.max(axis=1, keepdims=True)) * scale
            probs = [jnp.exp2(s * scale - top) for s in scores]
            last = jnp.exp2(last * scale - top)
            total = sum(probs).sum(axis=1, keepdims=True) + last.sum(axis=1, keepdims=True)
            probs = [p.astype(BF16) for p in probs]
            last = last.astype(BF16)
            halves = []
            for side in range(2):
                context = dot(last, sufs[layer][suffix_rows, side * hw : (side + 1) * hw])
                for q in range(QUARTERS):
                    context = context + dot(probs[q], (ka, kb)[side][q, r, :, :hw])
                halves.append(context)
            inverse = 1.0 / total
            context = jnp.concatenate([(h * inverse).astype(BF16) for h in halves], axis=1)
            for j in range(2):
                h = hp * 2 + j
                out[layer, suffix_rows, pl.ds(pl.multiple_of(h * dv, dv), dv)] = dot(
                    context[j * suffix : (j + 1) * suffix], wv[layer, h]
                ).astype(BF16)
            return carry

        lax.fori_loop(begin, end, one, 0)

    mid = pairs // 2
    for at in (8, 9, 10):
        loads[at].wait()
    if last_hop > 1:
        suffix_forward(1)
    absorb(0)
    if last_hop > 2:
        suffix_forward(2)
    loads[6].wait()
    loads[7].wait()
    fill(2)
    fill(3)
    plane_wait(0)
    compact(0)
    ring_send(0, 0)
    ring_send(0, 1)
    plane_send(2)
    suffix_forward(last_hop)
    absorb(1)
    plane_wait(1)
    compact(1)
    ring_send(1, 0)
    ring_send(1, 1)
    plane_send(3)
    forward(0, 0)
    forward(0, 1)
    suffix_wait(last_hop)
    loads[11].wait()
    forward(1, 0)
    plane_wait(2)
    compact(2)
    ring_send(2, 0)
    forward(1, 1)
    plane_wait(3)
    compact(3)
    ring_send(3, 0)
    ring_send(2, 1)
    ring_send(3, 1)
    arrived(0, 0)
    arrived(1, 0)
    attend(0, 0, 0, mid)
    forward(2, 0)
    attend(0, 0, mid, pairs)
    forward(3, 0)
    arrived(0, 1)
    arrived(1, 1)
    attend(0, 1, 0, mid)
    forward(2, 1)
    attend(0, 1, mid, pairs)
    forward(3, 1)
    arrived(2, 0)
    arrived(3, 0)
    attend(1, 0, 0, pairs)
    arrived(2, 1)
    arrived(3, 1)
    attend(1, 1, 0, pairs)

    for c in range(4):
        pltpu.make_async_copy(others(sends[c]), others(sends[c]), xy_send.at[c]).wait()
        for r in range(requests):
            for way in range(2):
                hop1(c, r, way).wait_send()
                hop2(c, r, way).wait_send()
    for h in range(last_hop + 1):
        for way in range(2):
            for layer in carried(h, way):
                suffix_copy(h, way, layer, False).wait_send()


def per_device(
    queries_nope,
    queries_rope,
    w_key,
    w_value,
    suffix_latent,
    suffix_rope,
    pool_latent,
    pool_rope,
    block_holders,
    block_ids,
    prefix_blocks,
):
    groups = lax.axis_size("group")
    tps = lax.axis_size("tp")
    requests, blocks = block_holders.shape[1:]
    layers, tokens = queries_nope.shape[:2]
    suffix = tokens // requests
    heads, dn, dc = w_key.shape[1:]
    dv = w_value.shape[3]
    dr = suffix_rope.shape[2]
    held, length = pool_latent.shape[1:3]
    piece = length // QUARTERS
    seg = blocks * piece
    rows = suffix_latent.shape[1]
    dims = (groups, tps, requests, blocks, suffix, heads, dc, dr, dn, dv)
    smem = pl.BlockSpec(memory_space=pltpu.SMEM)
    hbm = pl.BlockSpec(memory_space=pl.ANY)
    hw = dc // 2
    widths = (hw, hw + 2 * dr, hw, hw)
    units = 4 * requests
    landing = [pltpu.VMEM((groups, CAP, piece, w), BF16) for w in widths]
    hops = tps // 2
    return pl.pallas_call(
        functools.partial(kernel, dims),
        out_shape=jax.ShapeDtypeStruct((layers, tokens, heads * dv), BF16),
        in_specs=[smem] * 3 + [hbm] * 8,
        out_specs=pl.BlockSpec(memory_space=pltpu.VMEM),
        scratch_shapes=[
            pltpu.VMEM(queries_nope.shape, BF16),
            pltpu.VMEM(queries_rope.shape, BF16),
            pltpu.VMEM(w_key.shape, BF16),
            pltpu.VMEM(w_value.shape, BF16),
            [pltpu.VMEM((held, piece, hw), BF16) for _ in range(4)],
            pltpu.VMEM((layers, held, piece * dr), BF16),
            pltpu.VMEM((held, piece, 2 * dr), F32),
            pltpu.VMEM((held, piece, 2 * dr), BF16),
            pltpu.VMEM((layers, rows, dr), BF16),
            landing,
            landing,
            [pltpu.VMEM((QUARTERS, requests, seg, w), BF16) for w in widths],
            [pltpu.VMEM((rows * tps, w), BF16) for w in (dc + 2 * dr, dc)],
            pltpu.VMEM((layers, requests, heads // 2, 2 * suffix, dc), BF16),
            pltpu.VMEM((layers, requests, heads // 2, 2 * suffix, 2 * dr), BF16),
            pltpu.SMEM((groups, CAP), jnp.int32),
            pltpu.SMEM((requests, blocks), jnp.int32),
            pltpu.SemaphoreType.DMA((12,)),
            pltpu.SemaphoreType.DMA((4,)),
            pltpu.SemaphoreType.DMA((4,)),
            pltpu.SemaphoreType.DMA((hops, 2, 2)),
            pltpu.SemaphoreType.DMA((hops, 2, 2)),
            pltpu.SemaphoreType.DMA((units, 2)),
            pltpu.SemaphoreType.DMA((units, 2)),
            pltpu.SemaphoreType.DMA((units, 2)),
            pltpu.SemaphoreType.DMA((units, 2)),
        ],
        compiler_params=pltpu.CompilerParams(
            collective_id=0, has_side_effects=True, vmem_limit_bytes=56 * 1024 * 1024
        ),
        cost_estimate=pl.CostEstimate(
            flops=12_000_000_000, bytes_accessed=12_000_000, transcendentals=5_000_000
        ),
    )(
        block_holders,
        block_ids,
        prefix_blocks,
        queries_nope,
        queries_rope,
        w_key,
        w_value,
        suffix_latent,
        suffix_rope,
        pool_latent,
        pool_rope,
    )


def solution(mesh):
    in_specs = (
        P(None, "group", "tp"),
        P(None, "group", "tp"),
        P(None, "tp", None, None),
        P(None, "tp", None, None),
        P(None, ("group", "tp"), None),
        P(None, ("group", "tp"), None),
        P(None, "group", None, None),
        P(None, "group", None),
        P(),
        P(),
        P(),
    )
    out_specs = P(None, "group", "tp")
    return jax.shard_map(
        per_device, mesh=mesh, in_specs=in_specs, out_specs=out_specs, check_vma=False
    )
```

```python
import functools
import math

import jax
import jax.numpy as jnp
from jax import lax
from jax.experimental import pallas as pl
from jax.experimental.pallas import tpu as pltpu
from jax.sharding import PartitionSpec as P

MESH = pl.DeviceIdType.MESH
BF16 = jnp.bfloat16
F32 = jnp.float32
CAP = 2
QUARTERS = 4


def dot(a, b):
    return jnp.dot(a, b, preferred_element_type=F32)


def dot_t(a, b):
    return lax.dot_general(a, b, (((1,), (1,)), ((), ())), preferred_element_type=F32)


def torus_peer(g_me, groups, i):
    if groups != 32:
        return lax.rem(g_me + i, groups)
    x, y, c = g_me // 8, lax.rem(g_me // 2, 4), lax.rem(g_me, 2)
    x = lax.rem(x + i, 4)
    y = lax.rem(y + i + i // 4, 4)
    c = lax.rem(c + i // 16, 2)
    return x * 8 + y * 2 + c


def kernel(
    dims,
    holders,
    block_ids,
    prefix_blocks,
    qn_in,
    qr_in,
    wk_in,
    wv_in,
    sl_in,
    sr_in,
    pool_in,
    prope_in,
    out,
    qn,
    qr,
    wk,
    wv,
    pools,
    prope_lanes,
    prope_wide,
    prope,
    srope,
    sends,
    gots,
    keys,
    sufs,
    absorbed0,
    absorbed1,
    held_top,
    held_total,
    held_context,
    picks,
    ranks,
    in_sem,
    xy_send,
    xy_recv,
    suf_send,
    suf_recv,
    hop1_send,
    hop1_recv,
    hop2_send,
    hop2_recv,
):
    groups, tps, requests, blocks, suffix, heads, dc, dr, dn, dv = dims
    g_me = lax.axis_index("group")
    t_me = lax.axis_index("tp")
    right = lax.rem(t_me + 1, tps)
    left = lax.rem(t_me + tps - 1, tps)
    quarter = lax.rem(t_me, QUARTERS)
    q_left = lax.rem(quarter + QUARTERS - 1, QUARTERS)
    q_right = lax.rem(quarter + 1, QUARTERS)
    q_far = lax.rem(quarter + 2, QUARTERS)
    piece = 16
    widths = (dc // 4, dc // 4 + 2 * dr, dc // 2, dc // 2, dc // 2)
    places = (0, dc // 4, dc // 2 + 2 * dr, 0, dc // 2)
    whole = pl.ds(0, blocks * piece)
    seg = blocks * piece
    half = seg // 2
    rows = requests * suffix // tps
    pairs = heads // 2
    layers = 2
    hw = dc // 2
    qw = dc // 4
    rw = 2 * dr
    final = 4
    scale = math.log2(math.e) / math.sqrt(dn + dr)

    first = pl.multiple_of(quarter * piece, piece)
    lanes = pl.ds(pl.multiple_of(quarter * piece * dr, piece * dr), piece * dr)
    tokens = pl.ds(first, piece)
    far = pl.ds(pl.multiple_of(q_far * piece, piece), piece)
    mine = pl.ds(pl.multiple_of(t_me * rows, rows), rows)
    loads = [
        pltpu.make_async_copy(pool_in.at[0, :, tokens, pl.ds(0, qw)], pools[0], in_sem.at[0]),
        pltpu.make_async_copy(sl_in.at[0, :, pl.ds(0, hw)], sufs[0].at[mine, pl.ds(0, hw)], in_sem.at[1]),
        pltpu.make_async_copy(
            sl_in.at[0, :, pl.ds(hw, hw)], sufs[0].at[mine, pl.ds(hw + rw, hw)], in_sem.at[2]
        ),
        pltpu.make_async_copy(sl_in.at[1], sufs[1].at[mine, pl.ds(0, dc)], in_sem.at[3]),
        pltpu.make_async_copy(sr_in, srope, in_sem.at[4]),
        pltpu.make_async_copy(pool_in.at[0, :, tokens, pl.ds(qw, qw)], pools[1], in_sem.at[5]),
        pltpu.make_async_copy(prope_in.at[:, :, lanes], prope_lanes, in_sem.at[6]),
        pltpu.make_async_copy(pool_in.at[0, :, tokens, pl.ds(hw, hw)], pools[2], in_sem.at[7]),
        pltpu.make_async_copy(pool_in.at[1, :, tokens, pl.ds(0, hw)], pools[3], in_sem.at[8]),
        pltpu.make_async_copy(qn_in, qn, in_sem.at[9]),
        pltpu.make_async_copy(wk_in, wk, in_sem.at[10]),
        pltpu.make_async_copy(qr_in, qr, in_sem.at[11]),
        pltpu.make_async_copy(pool_in.at[1, :, tokens, pl.ds(hw, hw)], pools[4], in_sem.at[12]),
        pltpu.make_async_copy(pool_in.at[1, :, far, pl.ds(hw, hw)], pools[5], in_sem.at[13]),
        pltpu.make_async_copy(wv_in, wv, in_sem.at[14]),
    ]
    for load in loads:
        load.start()

    barrier = pltpu.get_barrier_semaphore()

    def greet(i, carry):
        pl.semaphore_signal(
            barrier, inc=1, device_id={"group": torus_peer(g_me, groups, i)}, device_id_type=MESH
        )
        return carry

    for neighbour in (left, right):
        pl.semaphore_signal(barrier, inc=1, device_id={"tp": neighbour}, device_id_type=MESH)
    lax.fori_loop(1, groups, greet, 0)

    slots = [(r, j) for r in range(requests) for j in range(blocks)]

    def table(g):
        names = [block_ids[r, j, g] for r, j in slots]
        own = [holders[r, j, g] == g_me for r, j in slots]
        late = g_me * 0
        for m, v in zip(own, names):
            late = jnp.where(m, v, late)
        early = late
        for m, v in zip(own[::-1], names[::-1]):
            early = jnp.where(m, v, early)
        picks[g, 0] = early
        picks[g, 1] = late

    def fill_and_send(c):
        def one(i, carry):
            g = torus_peer(g_me, groups, i)
            if c == 0:
                table(g)
            for k in range(CAP):
                b = picks[g, k]
                if c == 1:
                    sends[c][g, k, :, :qw] = pools[c][b]
                    sends[c][g, k, :, qw:] = prope[b]
                elif c == final:
                    sends[c][g, k, :piece] = pools[c][b]
                    sends[c][g, k, piece:] = pools[c + 1][b]
                else:
                    sends[c][g, k] = pools[c][b]
            plane_copy(c, g).start()
            return carry

        lax.fori_loop(1, groups, one, 0)

    def plane_copy(c, g):
        return pltpu.make_async_remote_copy(
            src_ref=sends[c].at[g],
            dst_ref=gots[c].at[g_me],
            send_sem=xy_send.at[c],
            recv_sem=xy_recv.at[c],
            device_id={"group": g},
            device_id_type=MESH,
        )

    def others(ref):
        return ref.at[pl.ds(1, groups - 1)]

    def plane_wait(c):
        pltpu.make_async_copy(others(gots[c]), others(gots[c]), xy_recv.at[c]).wait()

    def suffix_copy(h, way, layer, arriving):
        step = h + 1 if arriving else h
        origin = lax.rem(t_me + (tps - step if way == 0 else step), tps)
        ref = sufs[layer].at[pl.ds(pl.multiple_of(origin * rows, rows), rows)]
        if layer == 1:
            ref = ref.at[:, pl.ds(0, dc)]
        return pltpu.make_async_remote_copy(
            src_ref=ref,
            dst_ref=ref,
            send_sem=suf_send.at[h, way, layer],
            recv_sem=suf_recv.at[h, way, layer],
            device_id={"tp": (right, left)[way]},
            device_id_type=MESH,
        )

    last_hop = tps // 2 - 1

    def carried(h, way):
        return (0, 1) if h < last_hop else (way,)

    def suffix_send(h):
        for way in range(2):
            for layer in carried(h, way):
                suffix_copy(h, way, layer, False).start()

    def suffix_wait(h):
        for way in range(2):
            for layer in carried(h, way):
                suffix_copy(h, way, layer, True).wait_recv()

    def suffix_forward(h):
        suffix_wait(h - 1)
        suffix_send(h)

    for at in range(5):
        loads[at].wait()
    sufs[0][mine, hw : hw + rw] = jnp.concatenate(
        [srope[0].astype(F32), srope[1].astype(F32)], axis=1
    ).astype(BF16)
    pl.semaphore_wait(barrier, groups + 1)
    suffix_send(0)
    fill_and_send(0)

    loads[5].wait()
    loads[6].wait()
    held = prope.shape[0]
    low = lax.broadcasted_iota(jnp.int32, (held, 2 * dr), 1) < dr
    for j in range(piece // 2):
        x0 = prope_lanes[0, :, 2 * dr * j : 2 * dr * (j + 1)].astype(F32)
        x1 = prope_lanes[1, :, 2 * dr * j : 2 * dr * (j + 1)].astype(F32)
        prope_wide[:, 2 * j, :] = jnp.where(low, x0, pltpu.roll(x1, dr, 1))
        prope_wide[:, 2 * j + 1, :] = jnp.where(low, pltpu.roll(x0, dr, 1), x1)
    prope[...] = prope_wide[...].astype(BF16)
    fill_and_send(1)

    own = [holders[r, j, g_me] for r, j in slots]
    for s, (r, j) in enumerate(slots):
        rank = jnp.int32(0)
        for h in own[:s]:
            rank = jnp.where(h == own[s], 1, rank)
        ranks[r, j] = rank
    for c in range(5):
        for k in range(CAP):
            gots[c][g_me, k] = jnp.zeros(gots[c].shape[2:], BF16)

    lane = lax.broadcasted_iota(jnp.int32, (suffix, 2 * dr), 1)

    def head_rows(h, n):
        return pl.ds(pl.multiple_of(h * suffix, suffix), n * suffix)

    def absorb(layer):
        def one(hp, carry):
            for j in range(2):
                at = pl.ds(pl.multiple_of((hp * 2 + j) * dn, dn), dn)
                a = dot(qn[layer, :, at], wk[layer, hp * 2 + j]).astype(BF16)
                for r in range(requests):
                    to = head_rows(hp * 2 + j, 1)
                    part = a[r * suffix : (r + 1) * suffix]
                    if layer == 0:
                        absorbed0[r, to, :hw] = part[:, :hw]
                        absorbed0[r, to, hw + rw :] = part[:, hw:]
                    else:
                        absorbed1[r, to, :dc] = part
            at = pl.ds(pl.multiple_of(hp * rw, rw), rw)
            for r in range(requests):
                both = qr[layer, r * suffix : (r + 1) * suffix, at].astype(F32)
                swapped = pltpu.roll(both, dr, 1)
                for j in range(2):
                    to = head_rows(hp * 2 + j, 1)
                    values = swapped if j != layer else both
                    if layer == 0:
                        absorbed0[r, to, hw : hw + rw] = jnp.where(lane < dr, values, 0.0).astype(BF16)
                    else:
                        absorbed1[r, to, dc:] = jnp.where(lane >= dr, values, 0.0).astype(BF16)
            return carry

        lax.fori_loop(0, pairs, one, 0)

    def compact(c):
        def one(b, carry):
            for r in range(requests):
                at = pl.ds(pl.multiple_of(b * piece, piece), piece)
                source, rank = holders[r, b, g_me], ranks[r, b]
                into = keys[(0, 0, 0, 1, 1)[c]]
                to = pl.ds(places[c], widths[c])
                if c == final:
                    into[quarter, r, at, to] = gots[c][source, rank, :piece]
                    into[q_far, r, at, to] = gots[c][source, rank, piece:]
                else:
                    into[quarter, r, at, to] = gots[c][source, rank]
            return carry

        lax.fori_loop(0, blocks, one, 0)

    def part(c, q, r, at):
        return keys[(0, 0, 0, 1, 1)[c]].at[q, r, at, pl.ds(places[c], widths[c])]

    def ring_copy(ref, hop, unit, way):
        sems = ((hop1_send, hop1_recv), (hop2_send, hop2_recv))[hop]
        return pltpu.make_async_remote_copy(
            src_ref=ref,
            dst_ref=ref,
            send_sem=sems[0].at[unit, way],
            recv_sem=sems[1].at[unit, way],
            device_id={"tp": (right, left)[way]},
            device_id_type=MESH,
        )

    def hop1(c, r, way):
        return ring_copy(part(c, quarter, r, whole), 0, c * requests + r, way)

    def hop1_in(c, r, way):
        return ring_copy(part(c, (q_left, q_right)[way], r, whole), 0, c * requests + r, way)

    def hop2(c, r, way):
        ref = part(c, (q_left, q_right)[way], r, pl.ds(way * half, half))
        return ring_copy(ref, 1, c * requests + r, way)

    def hop2_in(c, r, way):
        ref = part(c, q_far, r, pl.ds(way * half, half))
        return ring_copy(ref, 1, c * requests + r, way)

    def ring_send(c, r):
        for way in range(2):
            hop1(c, r, way).start()

    def forward(c, r):
        for way in range(2):
            hop1_in(c, r, way).wait_recv()
            if c != final:
                hop2(c, r, way).start()

    def arrived(c, r):
        for way in range(2):
            hop2_in(c, r, way).wait_recv()

    def attend(layer, r, quarters, with_suffix, first, last):
        all_rows = heads * suffix
        suffix_rows = slice(r * suffix, (r + 1) * suffix)
        key_at = lax.broadcasted_iota(jnp.int32, (all_rows, seg), 1)
        live_prefix = key_at < prefix_blocks[r, g_me] * piece
        a = (absorbed0, absorbed1)[layer].at[r]
        if layer == 0:
            sides = (slice(0, hw), slice(hw + rw, dc + rw))
            terms = sides + (slice(hw, hw + rw),)
        else:
            sides = (slice(0, hw), slice(hw, dc))
            terms = sides + (slice(dc, dc + rw),)

        def score(k):
            return sum(dot_t(a[:, t], k[:, t]) for t in terms)

        scores = []
        for q in quarters:
            if layer == 1:
                keys[1][q, r, :, dc:] = keys[0][q, r, :, hw : hw + rw]
            scores.append(jnp.where(live_prefix, score(keys[layer].at[q, r]), -jnp.inf))
        values = [keys[layer].at[q, r] for q in quarters]
        if with_suffix:
            s = score(sufs[layer].at[suffix_rows])
            query_at = lax.rem(lax.broadcasted_iota(jnp.int32, s.shape, 0), suffix)
            live_suffix = lax.broadcasted_iota(jnp.int32, s.shape, 1) <= query_at
            scores.append(jnp.where(live_suffix, s, -jnp.inf))
            values.append(sufs[layer].at[suffix_rows])
        count = len(quarters)
        top = functools.reduce(jnp.maximum, scores[:count]).max(axis=1, keepdims=True)
        if with_suffix:
            top = jnp.maximum(top, scores[count].max(axis=1, keepdims=True))
        top = top * scale
        if not first:
            before = held_top[r]
            top = jnp.maximum(top, before)
            kept = jnp.exp2(before - top)
        probs = [jnp.exp2(s * scale - top) for s in scores]
        total = sum(probs[:count]).sum(axis=1, keepdims=True)
        if with_suffix:
            total = total + probs[count].sum(axis=1, keepdims=True)
        probs = [p.astype(BF16) for p in probs]
        contexts = [sum(dot(p, v[:, side]) for p, v in zip(probs, values)) for side in sides]
        if not first:
            total = total + held_total[r] * kept
            width = dc // len(sides)
            contexts = [
                c + held_context[r, :, i * width : (i + 1) * width] * kept
                for i, c in enumerate(contexts)
            ]
        if not last:
            held_top[r] = top
            held_total[r] = total
            for i, c in enumerate(contexts):
                held_context[r, :, i * c.shape[1] : (i + 1) * c.shape[1]] = c
            return
        inverse = 1.0 / total
        context = jnp.concatenate([(c * inverse).astype(BF16) for c in contexts], axis=1)
        for h in range(heads):
            out[layer, suffix_rows, h * dv : (h + 1) * dv] = dot(
                context[h * suffix : (h + 1) * suffix], wv[layer, h]
            ).astype(BF16)

    if last_hop > 1:
        suffix_forward(1)
    plane_wait(0)
    compact(0)
    ring_send(0, 0)
    ring_send(0, 1)
    loads[7].wait()
    fill_and_send(2)
    if last_hop > 2:
        suffix_forward(2)
    for at in (9, 10, 11):
        loads[at].wait()
    absorb(0)
    plane_wait(1)
    compact(1)
    ring_send(1, 0)
    ring_send(1, 1)
    suffix_forward(last_hop)
    forward(0, 0)
    forward(0, 1)
    loads[8].wait()
    fill_and_send(3)
    plane_wait(2)
    compact(2)
    ring_send(2, 0)
    ring_send(2, 1)
    forward(1, 0)
    forward(1, 1)
    loads[12].wait()
    loads[13].wait()
    fill_and_send(final)
    absorb(1)
    suffix_wait(last_hop)
    sufs[1][:, dc:] = sufs[0][:, hw : hw + rw]
    loads[14].wait()
    plane_wait(3)
    compact(3)
    forward(2, 0)
    forward(2, 1)
    ring_send(3, 0)
    ring_send(3, 1)
    for c in range(3):
        arrived(c, 0)
    attend(0, 0, range(QUARTERS), True, True, True)
    forward(3, 0)
    forward(3, 1)
    plane_wait(final)
    compact(final)
    ring_send(final, 0)
    ring_send(final, 1)
    for c in range(3):
        arrived(c, 1)
    attend(0, 1, range(QUARTERS), True, True, True)
    for r in range(requests):
        arrived(3, r)
        forward(final, r)
        attend(1, r, range(QUARTERS), True, True, True)

    for c in range(5):
        pltpu.make_async_copy(others(sends[c]), others(sends[c]), xy_send.at[c]).wait()
        for r in range(requests):
            for way in range(2):
                hop1(c, r, way).wait_send()
                if c != final:
                    hop2(c, r, way).wait_send()
    for h in range(last_hop + 1):
        for way in range(2):
            for layer in carried(h, way):
                suffix_copy(h, way, layer, False).wait_send()


def per_device(
    queries_nope,
    queries_rope,
    w_key,
    w_value,
    suffix_latent,
    suffix_rope,
    pool_latent,
    pool_rope,
    block_holders,
    block_ids,
    prefix_blocks,
):
    groups = lax.axis_size("group")
    tps = lax.axis_size("tp")
    requests, blocks = block_holders.shape[1:]
    layers, tokens = queries_nope.shape[:2]
    suffix = tokens // requests
    heads, dn, dc = w_key.shape[1:]
    dv = w_value.shape[3]
    dr = suffix_rope.shape[2]
    held, length = pool_latent.shape[1:3]
    piece = length // QUARTERS
    seg = blocks * piece
    rows = suffix_latent.shape[1]
    dims = (groups, tps, requests, blocks, suffix, heads, dc, dr, dn, dv)
    smem = pl.BlockSpec(memory_space=pltpu.SMEM)
    hbm = pl.BlockSpec(memory_space=pl.ANY)
    hw = dc // 2
    qw = dc // 4
    rw = 2 * dr
    final = 4
    qw = dc // 4
    rw = 2 * dr
    widths = (qw, qw + rw, hw, hw, hw)
    units = 5 * requests
    depths = (piece, piece, piece, piece, 2 * piece)
    landing = [pltpu.VMEM((groups, CAP, d, w), BF16) for d, w in zip(depths, widths)]
    hops = tps // 2
    return pl.pallas_call(
        functools.partial(kernel, dims),
        out_shape=pltpu.VMEM((layers, tokens, heads * dv), BF16),
        in_specs=[smem] * 3 + [hbm] * 8,
        out_specs=pl.BlockSpec(memory_space=pltpu.VMEM),
        scratch_shapes=[
            pltpu.VMEM(queries_nope.shape, BF16),
            pltpu.VMEM(queries_rope.shape, BF16),
            pltpu.VMEM(w_key.shape, BF16),
            pltpu.VMEM(w_value.shape, BF16),
            [pltpu.VMEM((held, piece, w), BF16) for w in (qw, qw, hw, hw, hw, hw)],
            pltpu.VMEM((layers, held, piece * dr), BF16),
            pltpu.VMEM((held, piece, 2 * dr), F32),
            pltpu.VMEM((held, piece, 2 * dr), BF16),
            pltpu.VMEM((layers, rows, dr), BF16),
            landing,
            landing,
            [pltpu.VMEM((QUARTERS, requests, seg, dc + rw), BF16) for _ in range(2)],
            [pltpu.VMEM((rows * tps, dc + rw), BF16) for _ in range(2)],
            pltpu.VMEM((requests, heads * suffix, dc + rw), BF16),
            pltpu.VMEM((requests, heads * suffix, dc + rw), BF16),
            pltpu.VMEM((requests, heads * suffix, 1), F32),
            pltpu.VMEM((requests, heads * suffix, 1), F32),
            pltpu.VMEM((requests, heads * suffix, dc), F32),
            pltpu.SMEM((groups, CAP), jnp.int32),
            pltpu.SMEM((requests, blocks), jnp.int32),
            pltpu.SemaphoreType.DMA((15,)),
            pltpu.SemaphoreType.DMA((5,)),
            pltpu.SemaphoreType.DMA((5,)),
            pltpu.SemaphoreType.DMA((hops, 2, 2)),
            pltpu.SemaphoreType.DMA((hops, 2, 2)),
            pltpu.SemaphoreType.DMA((units, 2)),
            pltpu.SemaphoreType.DMA((units, 2)),
            pltpu.SemaphoreType.DMA((units, 2)),
            pltpu.SemaphoreType.DMA((units, 2)),
        ],
        compiler_params=pltpu.CompilerParams(
            collective_id=0, has_side_effects=True, vmem_limit_bytes=56 * 1024 * 1024
        ),
        cost_estimate=pl.CostEstimate(
            flops=12_000_000_000, bytes_accessed=12_000_000, transcendentals=5_000_000
        ),
    )(
        block_holders.transpose(1, 2, 0),
        block_ids.transpose(1, 2, 0),
        prefix_blocks.T,
        queries_nope,
        queries_rope,
        w_key,
        w_value,
        suffix_latent,
        suffix_rope,
        pool_latent,
        pool_rope,
    )


def solution(mesh):
    in_specs = (
        P(None, "group", "tp"),
        P(None, "group", "tp"),
        P(None, "tp", None, None),
        P(None, "tp", None, None),
        P(None, ("group", "tp"), None),
        P(None, ("group", "tp"), None),
        P(None, "group", None, None),
        P(None, "group", None),
        P(),
        P(),
        P(),
    )
    out_specs = P(None, "group", "tp")
    return jax.shard_map(
        per_device, mesh=mesh, in_specs=in_specs, out_specs=out_specs, check_vma=False
    )
```

```python
import functools
import math

import jax
import jax.numpy as jnp
from jax import lax
from jax.experimental import pallas as pl
from jax.experimental.pallas import tpu as pltpu
from jax.sharding import PartitionSpec as P

MESH = pl.DeviceIdType.MESH
BF16 = jnp.bfloat16
F32 = jnp.float32
CAP = 2
QUARTERS = 4


def dot(a, b):
    return jnp.dot(a, b, preferred_element_type=F32)


def dot_t(a, b):
    return lax.dot_general(a, b, (((1,), (1,)), ((), ())), preferred_element_type=F32)


def torus_peer(g_me, groups, i):
    if groups != 32:
        return lax.rem(g_me + i, groups)
    x, y, c = g_me // 8, lax.rem(g_me // 2, 4), lax.rem(g_me, 2)
    x = lax.rem(x + i, 4)
    y = lax.rem(y + i + i // 4, 4)
    c = lax.rem(c + i // 16, 2)
    return x * 8 + y * 2 + c


def kernel(
    dims,
    holders,
    block_ids,
    prefix_blocks,
    qn_in,
    qr_in,
    wk_in,
    wv_in,
    sl_in,
    sr_in,
    pool_in,
    prope_in,
    out,
    qn,
    qr,
    wk,
    wv,
    pools,
    prope_lanes,
    prope_wide,
    prope,
    srope,
    sends,
    gots,
    keys,
    sufs,
    absorbed0,
    absorbed1,
    held_top,
    held_total,
    held_context,
    picks,
    ranks,
    in_sem,
    xy_send,
    xy_recv,
    suf_send,
    suf_recv,
    hop1_send,
    hop1_recv,
    hop2_send,
    hop2_recv,
):
    groups, tps, requests, blocks, suffix, heads, dc, dr, dn, dv = dims
    g_me = lax.axis_index("group")
    t_me = lax.axis_index("tp")
    right = lax.rem(t_me + 1, tps)
    left = lax.rem(t_me + tps - 1, tps)
    quarter = lax.rem(t_me, QUARTERS)
    q_left = lax.rem(quarter + QUARTERS - 1, QUARTERS)
    q_right = lax.rem(quarter + 1, QUARTERS)
    q_far = lax.rem(quarter + 2, QUARTERS)
    piece = 16
    widths = (dc // 4, dc // 4 + 2 * dr, dc // 2, dc // 2, dc // 2)
    places = (0, dc // 4, dc // 2 + 2 * dr, 0, dc // 2)
    whole = pl.ds(0, blocks * piece)
    seg = blocks * piece
    half = seg // 2
    rows = requests * suffix // tps
    pairs = heads // 2
    layers = 2
    hw = dc // 2
    qw = dc // 4
    rw = 2 * dr
    final = 4
    doubled = 3
    scale = math.log2(math.e) / math.sqrt(dn + dr)

    first = pl.multiple_of(quarter * piece, piece)
    lanes = pl.ds(pl.multiple_of(quarter * piece * dr, piece * dr), piece * dr)
    tokens = pl.ds(first, piece)
    far = pl.ds(pl.multiple_of(q_far * piece, piece), piece)
    mine = pl.ds(pl.multiple_of(t_me * rows, rows), rows)
    loads = [
        pltpu.make_async_copy(pool_in.at[0, :, tokens, pl.ds(0, qw)], pools[0], in_sem.at[0]),
        pltpu.make_async_copy(sl_in.at[0, :, pl.ds(0, hw)], sufs[0].at[mine, pl.ds(0, hw)], in_sem.at[1]),
        pltpu.make_async_copy(
            sl_in.at[0, :, pl.ds(hw, hw)], sufs[0].at[mine, pl.ds(hw + rw, hw)], in_sem.at[2]
        ),
        pltpu.make_async_copy(sl_in.at[1], sufs[1].at[mine, pl.ds(0, dc)], in_sem.at[3]),
        pltpu.make_async_copy(sr_in, srope, in_sem.at[4]),
        pltpu.make_async_copy(pool_in.at[0, :, tokens, pl.ds(qw, qw)], pools[1], in_sem.at[5]),
        pltpu.make_async_copy(prope_in.at[:, :, lanes], prope_lanes, in_sem.at[6]),
        pltpu.make_async_copy(pool_in.at[0, :, tokens, pl.ds(hw, hw)], pools[2], in_sem.at[7]),
        pltpu.make_async_copy(pool_in.at[1, :, tokens, pl.ds(0, hw)], pools[3], in_sem.at[8]),
        pltpu.make_async_copy(qn_in, qn, in_sem.at[9]),
        pltpu.make_async_copy(wk_in, wk, in_sem.at[10]),
        pltpu.make_async_copy(qr_in, qr, in_sem.at[11]),
        pltpu.make_async_copy(pool_in.at[1, :, tokens, pl.ds(hw, hw)], pools[4], in_sem.at[12]),
        pltpu.make_async_copy(pool_in.at[1, :, far, pl.ds(hw, hw)], pools[6], in_sem.at[13]),
        pltpu.make_async_copy(wv_in, wv, in_sem.at[14]),
        pltpu.make_async_copy(pool_in.at[1, :, far, pl.ds(0, hw)], pools[5], in_sem.at[15]),
    ]
    for load in loads:
        load.start()

    barrier = pltpu.get_barrier_semaphore()

    def greet(i, carry):
        pl.semaphore_signal(
            barrier, inc=1, device_id={"group": torus_peer(g_me, groups, i)}, device_id_type=MESH
        )
        return carry

    for neighbour in (left, right):
        pl.semaphore_signal(barrier, inc=1, device_id={"tp": neighbour}, device_id_type=MESH)
    lax.fori_loop(1, groups, greet, 0)

    slots = [(r, j) for r in range(requests) for j in range(blocks)]

    def table(g):
        names = [block_ids[r, j, g] for r, j in slots]
        own = [holders[r, j, g] == g_me for r, j in slots]
        late = g_me * 0
        for m, v in zip(own, names):
            late = jnp.where(m, v, late)
        early = late
        for m, v in zip(own[::-1], names[::-1]):
            early = jnp.where(m, v, early)
        picks[g, 0] = early
        picks[g, 1] = late

    def fill_and_send(c):
        def one(i, carry):
            g = torus_peer(g_me, groups, i)
            if c == 0:
                table(g)
            for k in range(CAP):
                b = picks[g, k]
                if c == 1:
                    sends[c][g, k, :, :qw] = pools[c][b]
                    sends[c][g, k, :, qw:] = prope[b]
                elif c >= doubled:
                    sends[c][g, k, :piece] = pools[c][b]
                    sends[c][g, k, piece:] = pools[c + 2][b]
                else:
                    sends[c][g, k] = pools[c][b]
            plane_copy(c, g).start()
            return carry

        lax.fori_loop(1, groups, one, 0)

    def plane_copy(c, g):
        return pltpu.make_async_remote_copy(
            src_ref=sends[c].at[g],
            dst_ref=gots[c].at[g_me],
            send_sem=xy_send.at[c],
            recv_sem=xy_recv.at[c],
            device_id={"group": g},
            device_id_type=MESH,
        )

    def others(ref):
        return ref.at[pl.ds(1, groups - 1)]

    def plane_wait(c):
        pltpu.make_async_copy(others(gots[c]), others(gots[c]), xy_recv.at[c]).wait()

    def suffix_copy(h, way, layer, arriving):
        step = h + 1 if arriving else h
        origin = lax.rem(t_me + (tps - step if way == 0 else step), tps)
        ref = sufs[layer].at[pl.ds(pl.multiple_of(origin * rows, rows), rows)]
        if layer == 1:
            ref = ref.at[:, pl.ds(0, dc)]
        return pltpu.make_async_remote_copy(
            src_ref=ref,
            dst_ref=ref,
            send_sem=suf_send.at[h, way, layer],
            recv_sem=suf_recv.at[h, way, layer],
            device_id={"tp": (right, left)[way]},
            device_id_type=MESH,
        )

    last_hop = tps // 2 - 1

    def carried(h, way):
        return (0, 1) if h < last_hop else (way,)

    def suffix_send(h):
        for way in range(2):
            for layer in carried(h, way):
                suffix_copy(h, way, layer, False).start()

    def suffix_wait(h):
        for way in range(2):
            for layer in carried(h, way):
                suffix_copy(h, way, layer, True).wait_recv()

    def suffix_forward(h):
        suffix_wait(h - 1)
        suffix_send(h)

    for at in range(5):
        loads[at].wait()
    sufs[0][mine, hw : hw + rw] = jnp.concatenate(
        [srope[0].astype(F32), srope[1].astype(F32)], axis=1
    ).astype(BF16)
    pl.semaphore_wait(barrier, groups + 1)
    suffix_send(0)
    fill_and_send(0)

    loads[5].wait()
    loads[6].wait()
    held = prope.shape[0]
    low = lax.broadcasted_iota(jnp.int32, (held, 2 * dr), 1) < dr
    for j in range(piece // 2):
        x0 = prope_lanes[0, :, 2 * dr * j : 2 * dr * (j + 1)].astype(F32)
        x1 = prope_lanes[1, :, 2 * dr * j : 2 * dr * (j + 1)].astype(F32)
        prope_wide[:, 2 * j, :] = jnp.where(low, x0, pltpu.roll(x1, dr, 1))
        prope_wide[:, 2 * j + 1, :] = jnp.where(low, pltpu.roll(x0, dr, 1), x1)
    prope[...] = prope_wide[...].astype(BF16)
    fill_and_send(1)

    own = [holders[r, j, g_me] for r, j in slots]
    for s, (r, j) in enumerate(slots):
        rank = jnp.int32(0)
        for h in own[:s]:
            rank = jnp.where(h == own[s], 1, rank)
        ranks[r, j] = rank
    for c in range(5):
        for k in range(CAP):
            gots[c][g_me, k] = jnp.zeros(gots[c].shape[2:], BF16)

    lane = lax.broadcasted_iota(jnp.int32, (suffix, 2 * dr), 1)

    def head_rows(h, n):
        return pl.ds(pl.multiple_of(h * suffix, suffix), n * suffix)

    def absorb(layer):
        def one(hp, carry):
            for j in range(2):
                at = pl.ds(pl.multiple_of((hp * 2 + j) * dn, dn), dn)
                a = dot(qn[layer, :, at], wk[layer, hp * 2 + j]).astype(BF16)
                for r in range(requests):
                    to = head_rows(hp * 2 + j, 1)
                    part = a[r * suffix : (r + 1) * suffix]
                    if layer == 0:
                        absorbed0[r, to, :hw] = part[:, :hw]
                        absorbed0[r, to, hw + rw :] = part[:, hw:]
                    else:
                        absorbed1[r, to, :dc] = part
            at = pl.ds(pl.multiple_of(hp * rw, rw), rw)
            for r in range(requests):
                both = qr[layer, r * suffix : (r + 1) * suffix, at].astype(F32)
                swapped = pltpu.roll(both, dr, 1)
                for j in range(2):
                    to = head_rows(hp * 2 + j, 1)
                    values = swapped if j != layer else both
                    if layer == 0:
                        absorbed0[r, to, hw : hw + rw] = jnp.where(lane < dr, values, 0.0).astype(BF16)
                    else:
                        absorbed1[r, to, dc:] = jnp.where(lane >= dr, values, 0.0).astype(BF16)
            return carry

        lax.fori_loop(0, pairs, one, 0)

    def compact(c):
        def one(b, carry):
            for r in range(requests):
                at = pl.ds(pl.multiple_of(b * piece, piece), piece)
                source, rank = holders[r, b, g_me], ranks[r, b]
                into = keys[(0, 0, 0, 1, 1)[c]]
                to = pl.ds(places[c], widths[c])
                if c >= doubled:
                    into[quarter, r, at, to] = gots[c][source, rank, :piece]
                    into[q_far, r, at, to] = gots[c][source, rank, piece:]
                else:
                    into[quarter, r, at, to] = gots[c][source, rank]
            return carry

        lax.fori_loop(0, blocks, one, 0)

    def part(c, q, r, at):
        return keys[(0, 0, 0, 1, 1)[c]].at[q, r, at, pl.ds(places[c], widths[c])]

    def ring_copy(ref, hop, unit, way):
        sems = ((hop1_send, hop1_recv), (hop2_send, hop2_recv))[hop]
        return pltpu.make_async_remote_copy(
            src_ref=ref,
            dst_ref=ref,
            send_sem=sems[0].at[unit, way],
            recv_sem=sems[1].at[unit, way],
            device_id={"tp": (right, left)[way]},
            device_id_type=MESH,
        )

    def hop1(c, r, way):
        return ring_copy(part(c, quarter, r, whole), 0, c * requests + r, way)

    def hop1_in(c, r, way):
        return ring_copy(part(c, (q_left, q_right)[way], r, whole), 0, c * requests + r, way)

    def hop2(c, r, way):
        ref = part(c, (q_left, q_right)[way], r, pl.ds(way * half, half))
        return ring_copy(ref, 1, c * requests + r, way)

    def hop2_in(c, r, way):
        ref = part(c, q_far, r, pl.ds(way * half, half))
        return ring_copy(ref, 1, c * requests + r, way)

    def ring_send(c, r):
        for way in range(2):
            hop1(c, r, way).start()

    def forward(c, r):
        for way in range(2):
            hop1_in(c, r, way).wait_recv()
            if c < doubled:
                hop2(c, r, way).start()

    def arrived(c, r):
        for way in range(2):
            hop2_in(c, r, way).wait_recv()

    def attend(layer, r, quarters, with_suffix, first, last):
        all_rows = heads * suffix
        suffix_rows = slice(r * suffix, (r + 1) * suffix)
        key_at = lax.broadcasted_iota(jnp.int32, (all_rows, seg), 1)
        live_prefix = key_at < prefix_blocks[r, g_me] * piece
        a = (absorbed0, absorbed1)[layer].at[r]
        if layer == 0:
            sides = (slice(0, hw), slice(hw + rw, dc + rw))
            terms = sides + (slice(hw, hw + rw),)
        else:
            sides = (slice(0, hw), slice(hw, dc))
            terms = sides + (slice(dc, dc + rw),)

        def score(k):
            return sum(dot_t(a[:, t], k[:, t]) for t in terms)

        scores = []
        for q in quarters:
            if layer == 1:
                keys[1][q, r, :, dc:] = keys[0][q, r, :, hw : hw + rw]
            scores.append(jnp.where(live_prefix, score(keys[layer].at[q, r]), -jnp.inf))
        values = [keys[layer].at[q, r] for q in quarters]
        if with_suffix:
            s = score(sufs[layer].at[suffix_rows])
            query_at = lax.rem(lax.broadcasted_iota(jnp.int32, s.shape, 0), suffix)
            live_suffix = lax.broadcasted_iota(jnp.int32, s.shape, 1) <= query_at
            scores.append(jnp.where(live_suffix, s, -jnp.inf))
            values.append(sufs[layer].at[suffix_rows])
        count = len(quarters)
        top = functools.reduce(jnp.maximum, scores[:count]).max(axis=1, keepdims=True)
        if with_suffix:
            top = jnp.maximum(top, scores[count].max(axis=1, keepdims=True))
        top = top * scale
        if not first:
            before = held_top[r]
            top = jnp.maximum(top, before)
            kept = jnp.exp2(before - top)
        probs = [jnp.exp2(s * scale - top) for s in scores]
        total = sum(probs[:count]).sum(axis=1, keepdims=True)
        if with_suffix:
            total = total + probs[count].sum(axis=1, keepdims=True)
        probs = [p.astype(BF16) for p in probs]
        contexts = [sum(dot(p, v[:, side]) for p, v in zip(probs, values)) for side in sides]
        if not first:
            total = total + held_total[r] * kept
            width = dc // len(sides)
            contexts = [
                c + held_context[r, :, i * width : (i + 1) * width] * kept
                for i, c in enumerate(contexts)
            ]
        if not last:
            held_top[r] = top
            held_total[r] = total
            for i, c in enumerate(contexts):
                held_context[r, :, i * c.shape[1] : (i + 1) * c.shape[1]] = c
            return
        inverse = 1.0 / total
        context = jnp.concatenate([(c * inverse).astype(BF16) for c in contexts], axis=1)
        for h in range(heads):
            out[layer, suffix_rows, h * dv : (h + 1) * dv] = dot(
                context[h * suffix : (h + 1) * suffix], wv[layer, h]
            ).astype(BF16)

    if last_hop > 1:
        suffix_forward(1)
    plane_wait(0)
    compact(0)
    ring_send(0, 0)
    ring_send(0, 1)
    loads[7].wait()
    fill_and_send(2)
    if last_hop > 2:
        suffix_forward(2)
    for at in (9, 10, 11):
        loads[at].wait()
    absorb(0)
    plane_wait(1)
    compact(1)
    ring_send(1, 0)
    ring_send(1, 1)
    suffix_forward(last_hop)
    forward(0, 0)
    forward(0, 1)
    loads[8].wait()
    loads[15].wait()
    fill_and_send(3)
    plane_wait(2)
    compact(2)
    ring_send(2, 0)
    ring_send(2, 1)
    forward(1, 0)
    forward(1, 1)
    loads[12].wait()
    loads[13].wait()
    fill_and_send(final)
    absorb(1)
    suffix_wait(last_hop)
    sufs[1][:, dc:] = sufs[0][:, hw : hw + rw]
    loads[14].wait()
    for r in range(requests):
        attend(0, r, (quarter,), True, True, False)
    plane_wait(3)
    compact(3)
    forward(2, 0)
    forward(2, 1)
    ring_send(3, 0)
    ring_send(3, 1)
    for r in range(requests):
        attend(0, r, (q_left, q_right), False, False, False)
    for r in range(requests):
        for c in range(3):
            arrived(c, r)
        attend(0, r, (q_far,), False, False, True)
    plane_wait(final)
    compact(final)
    ring_send(final, 0)
    ring_send(final, 1)
    for r in range(requests):
        attend(1, r, (quarter, q_far), True, True, False)
    for r in range(requests):
        forward(3, r)
        forward(final, r)
        attend(1, r, (q_left, q_right), False, False, True)

    for c in range(5):
        pltpu.make_async_copy(others(sends[c]), others(sends[c]), xy_send.at[c]).wait()
        for r in range(requests):
            for way in range(2):
                hop1(c, r, way).wait_send()
                if c < doubled:
                    hop2(c, r, way).wait_send()
    for h in range(last_hop + 1):
        for way in range(2):
            for layer in carried(h, way):
                suffix_copy(h, way, layer, False).wait_send()


def per_device(
    queries_nope,
    queries_rope,
    w_key,
    w_value,
    suffix_latent,
    suffix_rope,
    pool_latent,
    pool_rope,
    block_holders,
    block_ids,
    prefix_blocks,
):
    groups = lax.axis_size("group")
    tps = lax.axis_size("tp")
    requests, blocks = block_holders.shape[1:]
    layers, tokens = queries_nope.shape[:2]
    suffix = tokens // requests
    heads, dn, dc = w_key.shape[1:]
    dv = w_value.shape[3]
    dr = suffix_rope.shape[2]
    held, length = pool_latent.shape[1:3]
    piece = length // QUARTERS
    seg = blocks * piece
    rows = suffix_latent.shape[1]
    dims = (groups, tps, requests, blocks, suffix, heads, dc, dr, dn, dv)
    smem = pl.BlockSpec(memory_space=pltpu.SMEM)
    hbm = pl.BlockSpec(memory_space=pl.ANY)
    hw = dc // 2
    qw = dc // 4
    rw = 2 * dr
    final = 4
    doubled = 3
    qw = dc // 4
    rw = 2 * dr
    widths = (qw, qw + rw, hw, hw, hw)
    units = 5 * requests
    depths = (piece, piece, piece, 2 * piece, 2 * piece)
    landing = [pltpu.VMEM((groups, CAP, d, w), BF16) for d, w in zip(depths, widths)]
    hops = tps // 2
    return pl.pallas_call(
        functools.partial(kernel, dims),
        out_shape=pltpu.VMEM((layers, tokens, heads * dv), BF16),
        in_specs=[smem] * 3 + [hbm] * 8,
        out_specs=pl.BlockSpec(memory_space=pltpu.VMEM),
        scratch_shapes=[
            pltpu.VMEM(queries_nope.shape, BF16),
            pltpu.VMEM(queries_rope.shape, BF16),
            pltpu.VMEM(w_key.shape, BF16),
            pltpu.VMEM(w_value.shape, BF16),
            [pltpu.VMEM((held, piece, w), BF16) for w in (qw, qw, hw, hw, hw, hw, hw)],
            pltpu.VMEM((layers, held, piece * dr), BF16),
            pltpu.VMEM((held, piece, 2 * dr), F32),
            pltpu.VMEM((held, piece, 2 * dr), BF16),
            pltpu.VMEM((layers, rows, dr), BF16),
            landing,
            landing,
            [pltpu.VMEM((QUARTERS, requests, seg, dc + rw), BF16) for _ in range(2)],
            [pltpu.VMEM((rows * tps, dc + rw), BF16) for _ in range(2)],
            pltpu.VMEM((requests, heads * suffix, dc + rw), BF16),
            pltpu.VMEM((requests, heads * suffix, dc + rw), BF16),
            pltpu.VMEM((requests, heads * suffix, 1), F32),
            pltpu.VMEM((requests, heads * suffix, 1), F32),
            pltpu.VMEM((requests, heads * suffix, dc), F32),
            pltpu.SMEM((groups, CAP), jnp.int32),
            pltpu.SMEM((requests, blocks), jnp.int32),
            pltpu.SemaphoreType.DMA((16,)),
            pltpu.SemaphoreType.DMA((5,)),
            pltpu.SemaphoreType.DMA((5,)),
            pltpu.SemaphoreType.DMA((hops, 2, 2)),
            pltpu.SemaphoreType.DMA((hops, 2, 2)),
            pltpu.SemaphoreType.DMA((units, 2)),
            pltpu.SemaphoreType.DMA((units, 2)),
            pltpu.SemaphoreType.DMA((units, 2)),
            pltpu.SemaphoreType.DMA((units, 2)),
        ],
        compiler_params=pltpu.CompilerParams(
            collective_id=0, has_side_effects=True, vmem_limit_bytes=56 * 1024 * 1024
        ),
        cost_estimate=pl.CostEstimate(
            flops=12_000_000_000, bytes_accessed=12_000_000, transcendentals=5_000_000
        ),
    )(
        block_holders.transpose(1, 2, 0),
        block_ids.transpose(1, 2, 0),
        prefix_blocks.T,
        queries_nope,
        queries_rope,
        w_key,
        w_value,
        suffix_latent,
        suffix_rope,
        pool_latent,
        pool_rope,
    )


def solution(mesh):
    in_specs = (
        P(None, "group", "tp"),
        P(None, "group", "tp"),
        P(None, "tp", None, None),
        P(None, "tp", None, None),
        P(None, ("group", "tp"), None),
        P(None, ("group", "tp"), None),
        P(None, "group", None, None),
        P(None, "group", None),
        P(),
        P(),
        P(),
    )
    out_specs = P(None, "group", "tp")
    return jax.shard_map(
        per_device, mesh=mesh, in_specs=in_specs, out_specs=out_specs, check_vma=False
    )
```
